256 devices in a mesh: row: 32 (over z, y_lo, core), col: 8 (over y_hi, x).
Axes of the slice: x: 4, y: 4 (y_hi: 2, y_lo: 2; y = y_hi * 2 + y_lo), z: 8, core: 2. Of those that a mesh axis runs over, the one named last changes fastest.
Arguments:
- matrix: bfloat16 [6144, 6144], P('row', 'col'), may hold values from -1 to 1, as said below
- pattern: int32 [48, 48], replicated, may hold values 0 or 1
- keep: int32 [48, 48], replicated, may hold values 0 or 1
Outputs:
- updated: bfloat16 [6144, 6144], P('row', 'col')
The draws below stay inside these ranges and needn't reach their ends.
Inputs may be any that keep to these rules, and one draw needn't show every extreme that they name: matrix is symmetric, its diagonal entries of either sign and magnitude well above the off-diagonal ones.
All inputs are finite; a program needn't handle non-finite values.
Results may differ from the reference program's by a relative error of at most 0.0052.
Values may be sent and summed in bfloat16 or wider, within the bound.
No kernel may reach another device: no remote copies, remote signals or barrier semaphores. Data moves between devices by JAX's collectives and lax.ppermute only.
A program may use at most 64 MiB of HBM per device.

```python
import math
import jax
import jax.numpy as jnp
from jax import lax

BS = 128
ORDER = 6144
NB = 48


def draw_matrix(key, part):
    key = jax.random.fold_in(key, 11)
    first, second, third = jax.random.split(key, 3)
    base = jax.random.normal(first, (ORDER, ORDER), jnp.float32)
    scale = 1.0 / math.sqrt(2.0 * ORDER)
    offdiag = (base + base.T) * scale
    magnitude = jnp.exp(jax.random.uniform(second, (ORDER,), jnp.float32, math.log(0.2), math.log(0.8)))
    signs = jnp.where(jax.random.bernoulli(third, 0.5, (ORDER,)), 1.0, -1.0)
    eye_full = jnp.eye(ORDER, dtype=jnp.float32)
    whole = offdiag * (1.0 - eye_full) + eye_full * (magnitude * signs)[:, None]
    return whole.astype(jnp.bfloat16)


def plant(drawn, rng, smallest, top_value):
    place = [jax.random.randint(jax.random.fold_in(rng, axis), (), 0, length) for axis, length in enumerate(drawn.shape)]
    main_axis = drawn.shape.index(max(drawn.shape))
    beside = place[:main_axis] + [(place[main_axis] + 1) % drawn.shape[main_axis]] + place[main_axis + 1:]
    return drawn.at[tuple(place)].set(smallest).at[tuple(beside)].set(top_value)


def setup_inputs(seed: int = 0) -> dict:
    key_of = jax.random.split(jax.random.key(seed), 4)
    matrix = draw_matrix(jax.random.fold_in(key_of[3], 71), 0)
    pattern = plant((jax.random.randint(key_of[1], (NB, NB), 0, 2) < 1).astype(jnp.int32), jax.random.fold_in(key_of[1], 1), 0, 1)
    keep = plant((jax.random.randint(key_of[2], (NB, NB), 0, 4) < 3).astype(jnp.int32), jax.random.fold_in(key_of[2], 1), 0, 1)
    return {"matrix": matrix, "pattern": pattern, "keep": keep}


def full_mask(table, with_diagonal):
    upper = jnp.triu(table)
    sym = upper + jnp.triu(table, 1).T
    if with_diagonal:
        sym = jnp.maximum(sym, jnp.eye(table.shape[0], dtype=jnp.int32))
    block = (sym > 0).astype(jnp.float32)
    return jnp.repeat(jnp.repeat(block, BS, axis=0), BS, axis=1)


def reference(matrix, pattern, keep):
    smask = full_mask(pattern, True)
    kmask = full_mask(keep, False)
    xmat = (matrix.astype(jnp.float32) * smask).astype(jnp.bfloat16).astype(jnp.float32)
    square = jnp.dot(xmat, xmat, preferred_element_type=jnp.float32, precision=lax.Precision.HIGHEST)
    eye_full = jnp.eye(ORDER, dtype=jnp.float32)
    weight = (1.5 * eye_full - 0.5 * (square * kmask)).astype(jnp.bfloat16).astype(jnp.float32)
    result = jnp.dot(xmat, weight, preferred_element_type=jnp.float32, precision=lax.Precision.HIGHEST)
    return (result * smask).astype(jnp.bfloat16)
```

```python
import jax
import jax.numpy as jnp
import numpy as np
from jax import lax
from jax.experimental import pallas as pl
from jax.experimental.pallas import tpu as pltpu
from jax.sharding import PartitionSpec as P

SIZES = (8, 2, 2, 2, 4)
AXES = ("row", "col")
ROWS, COLS = 192, 768
HALF = COLS // 2
SLAB, BLOCK = 64, 128
VMEM_LIMIT = 48 * 1024 * 1024
F32, BF16 = jnp.float32, jnp.bfloat16


def moves(step):
    pairs = []
    for index, place in enumerate(np.ndindex(*SIZES)):
        target = np.mod(step(*place), SIZES)
        pairs.append((index, int(np.ravel_multi_index(target, SIZES))))
    return pairs


def along_y(shift):
    def step(z, yl, core, yh, x):
        y = (2 * yh + yl + shift) % 4
        return z, y % 2, core, y // 2, x

    return moves(step)


EAST = moves(lambda z, yl, core, yh, x: (z, yl, core, yh, x + 1))
WEST = moves(lambda z, yl, core, yh, x: (z, yl, core, yh, x - 1))
NORTH, SOUTH = along_y(1), along_y(-1)
ACROSS = moves(lambda z, yl, core, yh, x: (z, yl, core, yh + 1, x + 2))
TWIN = moves(lambda z, yl, core, yh, x: (z, 1 - yl, core, yh, x))
CORE = moves(lambda z, yl, core, yh, x: (z, yl, 1 - core, yh, x))
RING = moves(lambda z, yl, core, yh, x: (z + 1 - 2 * core, yl, core, yh, x))


def send(value, pairs):
    return lax.ppermute(value, AXES, pairs)


def cat(*parts):
    return jnp.concatenate(parts, axis=0)


def place():
    row, col = lax.axis_index("row"), lax.axis_index("col")
    return row // 4, (row // 2) % 2, row % 2, col


def listed(table, a, b):
    return table[jnp.minimum(a, b), jnp.maximum(a, b)] > 0


def mask_kernel(pattern, matrix, masked, keep, away):
    _, yl, _, col = place()
    row = lax.axis_index("row")
    for i in range(ROWS // SLAB):
        a = (row * 3 + i) // 2
        rows = slice(SLAB * i, SLAB * (i + 1))
        parts = []
        for j in range(COLS // BLOCK):
            b = col * 6 + j
            factor = jnp.where(listed(pattern, a, b) | (a == b), 1.0, 0.0).astype(F32)
            part = matrix[rows, BLOCK * j : BLOCK * (j + 1)].astype(F32) * factor
            parts.append(part.astype(BF16))
        line = jnp.concatenate(parts, axis=1)
        masked[rows, :] = line

    @pl.when(yl == 0)
    def _():
        keep[...] = masked[:, :HALF]
        away[...] = masked[:, HALF:]

    @pl.when(yl == 1)
    def _():
        keep[...] = masked[:, HALF:]
        away[...] = masked[:, :HALF]


OFFSETS = (
    (0, 0), (-1, 0), (1, 0), (0, -1), (0, 1),
    (-1, -1), (1, 1), (1, -1), (-1, 1),
    (2, 0), (0, 2), (-1, 2), (1, 2), (2, -1), (2, 1), (2, 2),
)


def fill_columns(column, pieces):
    own, other, low, low_other, high, far = pieces
    z, yl, core, _ = place()
    sign = 2 * core - 1

    def put(ref, start, k, which):
        k = lax.rem(k + 16, 8)
        column[k, yl * 2 + which] = ref[start : start + ROWS, :]
        column[k, (1 - yl) * 2 + which] = ref[start + ROWS : start + 2 * ROWS, :]

    put(own, 0, z, core)
    put(other, 0, z, 1 - core)
    for s in range(3):
        put(low[s], 0, z + sign * (s + 1), core)
        put(low_other[s], 0, z + sign * (s + 1), 1 - core)
        put(high[s], 0, z - sign * (s + 1), 1 - core)
        put(high[s], 2 * ROWS, z - sign * (s + 1), core)
    put(far[0], 0, z + 4, core)
    put(far[1], 0, z + 4, 1 - core)


def products(panel, column, total):
    total[...] = jnp.zeros_like(total)

    def step(k, carry):
        right = column[k].reshape(COLS, HALF)
        total[...] += jnp.dot(panel[k], right, preferred_element_type=F32)
        return carry

    lax.fori_loop(0, 8, step, 0)


def tiles(body):
    z, yl, core, col = place()
    for h in range(2):
        which = yl if h == 0 else 1 - yl
        slabs = (z * 4 + which * 2 + core) * 3
        for i in range(3):
            for j in range(3):
                a, b = (slabs + i) // 2, col * 6 + yl * 3 + j
                rows = slice(ROWS * h + SLAB * i, ROWS * h + SLAB * (i + 1))
                cols = slice(BLOCK * j, BLOCK * (j + 1))
                body(rows, cols, a, b, (slabs + i) * SLAB, b * BLOCK)


def split_pieces(refs):
    own, other, a1, b1, a2, b2, a3, b3, a4, s1, s2, s3, s4 = refs
    return own, other, (a1, a2, a3), (b1, b2, b3), (s1, s2, s3), (a4, s4)


def square_kernel(*refs):
    keep, blocks, pieces = refs[0], refs[1:17], refs[17:30]
    weight, panel, column, total = refs[30:]
    _, yl, _, col = place()
    yh, x = col // 4, col % 4
    for (dx, dy), ref in zip(OFFSETS, blocks, strict=True):
        x_from = lax.rem(x + dx + 4, 4)
        y_from = lax.rem(2 * yh + yl + dy + 4, 4)
        part = dy % 2
        panel[(y_from // 2) * 4 + x_from, ROWS * part : ROWS * (part + 1), :] = ref[...]
    fill_columns(column, split_pieces(pieces))
    products(panel, column, total)

    def body(rows, cols, a, b, row0, col0):
        factor = jnp.where(listed(keep, a, b), 0.5, 0.0).astype(F32)
        shape = (SLAB, BLOCK)
        down = lax.broadcasted_iota(jnp.int32, shape, 0) + row0
        over = lax.broadcasted_iota(jnp.int32, shape, 1) + col0
        eye = jnp.where(down == over, 1.5, 0.0).astype(F32)
        weight[rows, cols] = (eye - total[rows, cols] * factor).astype(BF16)

    tiles(body)


def update_kernel(*refs):
    pattern, panel, pieces = refs[0], refs[1], refs[2:15]
    mine, away, column, total = refs[15:]
    fill_columns(column, split_pieces(pieces))
    products(panel, column, total)

    def body(rows, cols, a, b, row0, col0):
        del row0, col0
        factor = jnp.where(listed(pattern, a, b) | (a == b), 1.0, 0.0).astype(F32)
        value = (total[rows, cols] * factor).astype(BF16)
        if rows.start < ROWS:
            mine[rows, cols] = value
        else:
            away[rows.start - ROWS : rows.stop - ROWS, cols] = value

    tiles(body)


SMEM, VMEM = (pl.BlockSpec(memory_space=space) for space in (pltpu.SMEM, pltpu.VMEM))


def struct(*shape, dtype=BF16):
    return jax.ShapeDtypeStruct(shape, dtype)


def call(kernel, args, outs, scratch, flops):
    return pl.pallas_call(
        kernel,
        in_specs=[SMEM] + [VMEM] * (len(args) - 1),
        out_specs=[VMEM] * len(outs),
        out_shape=outs,
        scratch_shapes=scratch,
        cost_estimate=pl.CostEstimate(flops=flops, bytes_accessed=0, transcendentals=0),
        compiler_params=pltpu.CompilerParams(vmem_limit_bytes=VMEM_LIMIT),
    )(*args)


def ring(piece):
    other = send(piece, CORE)
    a, b, got, swapped = piece, other, [], []
    for _ in range(3):
        a, b = send(a, RING), send(b, RING)
        got += [a, b]
        swapped.append(send(cat(a, b), CORE))
    a = send(a, RING)
    return [piece, other, *got, a, *swapped, send(a, CORE)]


def plane(x):
    half = ROWS // 2
    d = send(x, ACROSS)
    w, e, s, n = send(x, EAST), send(x, WEST), send(x, NORTH), send(x, SOUTH)
    sw = send(cat(s, w[:half]), EAST)
    ne = send(cat(n, e[half:]), WEST)
    se = send(cat(e, s[:half]), NORTH)
    nw = send(cat(w, n[half:]), SOUTH)
    x2 = cat(sw[ROWS:], ne[ROWS:])
    y2 = cat(se[ROWS:], nw[ROWS:])
    c1, c2, c3, c4 = send(y2, EAST), send(y2, WEST), send(x2, NORTH), send(x2, SOUTH)
    return [x, w, e, s, n, sw[:ROWS], ne[:ROWS], se[:ROWS], nw[:ROWS], x2, y2, c1, c2, c3, c4, d]


SCRATCH = [pltpu.VMEM((8, 4, ROWS, HALF), BF16), pltpu.VMEM((2 * ROWS, HALF), F32)]
FLOPS = 2 * 2 * ROWS * HALF * 6144


def shards(matrix, pattern, keep):
    _, yl, _, _ = place()
    x, kept, away = call(
        mask_kernel,
        [pattern, matrix],
        [struct(ROWS, COLS), struct(ROWS, HALF), struct(ROWS, HALF)],
        [],
        0,
    )
    pieces = ring(cat(kept, send(away, TWIN)))
    weight, panel = call(
        square_kernel,
        [keep, *plane(x), *pieces],
        [struct(2 * ROWS, HALF), struct(8, 2 * ROWS, COLS)],
        SCRATCH,
        FLOPS,
    )
    mine, away = call(
        update_kernel,
        [pattern, panel, *ring(weight)],
        [struct(ROWS, HALF), struct(ROWS, HALF)],
        SCRATCH,
        FLOPS,
    )
    theirs = send(away, TWIN)
    left, right = jnp.where(yl == 0, mine, theirs), jnp.where(yl == 0, theirs, mine)
    return jnp.concatenate([left, right], axis=1)


def solution(mesh):
    return jax.shard_map(
        shards,
        mesh=mesh,
        in_specs=(P("row", "col"), P(), P()),
        out_specs=P("row", "col"),
        check_vma=False,
    )
```

```python
import jax
import jax.numpy as jnp
import numpy as np
from jax import lax
from jax.experimental import pallas as pl
from jax.experimental.pallas import tpu as pltpu
from jax.sharding import PartitionSpec as P

SIZES = (8, 2, 2, 2, 4)
AXES = ("row", "col")
ROWS, COLS = 192, 768
HALF = COLS // 2
SLAB, BLOCK = 64, 128
VMEM_LIMIT = 18 * 1024 * 1024
F32, BF16 = jnp.float32, jnp.bfloat16


def moves(step):
    pairs = []
    for index, place in enumerate(np.ndindex(*SIZES)):
        target = np.mod(step(*place), SIZES)
        pairs.append((index, int(np.ravel_multi_index(target, SIZES))))
    return pairs


def along_y(sign):
    def step(z, yl, core, yh, x):
        y = (2 * yh + yl + sign) % 4
        return z, y % 2, core, y // 2, x

    return moves(step)


EAST = moves(lambda z, yl, core, yh, x: (z, yl, core, yh, x + 1))
WEST = moves(lambda z, yl, core, yh, x: (z, yl, core, yh, x - 1))
NORTH, SOUTH = along_y(1), along_y(-1)
ACROSS = moves(lambda z, yl, core, yh, x: (z, yl, core, 1 - yh, x))
TWIN = moves(lambda z, yl, core, yh, x: (z, 1 - yl, core, yh, x))
CORE = moves(lambda z, yl, core, yh, x: (z, yl, 1 - core, yh, x))
RING = moves(lambda z, yl, core, yh, x: (z + 1 - 2 * core, yl, core, yh, x))


def send(value, pairs):
    return lax.ppermute(value, AXES, pairs)


def cat(*parts):
    return jnp.concatenate(parts, axis=0)


def place():
    row, col = lax.axis_index("row"), lax.axis_index("col")
    return row // 4, (row // 2) % 2, row % 2, col


def listed(table, a, b):
    return table[jnp.minimum(a, b), jnp.maximum(a, b)] > 0


def mask_kernel(pattern, matrix, masked, keep, away):
    _, yl, _, col = place()
    row = lax.axis_index("row")
    for i in range(ROWS // SLAB):
        a = (row * 3 + i) // 2
        rows = slice(SLAB * i, SLAB * (i + 1))
        parts = []
        for j in range(COLS // BLOCK):
            b = col * 6 + j
            factor = jnp.where(listed(pattern, a, b) | (a == b), 1.0, 0.0).astype(F32)
            part = matrix[rows, BLOCK * j : BLOCK * (j + 1)].astype(F32) * factor
            parts.append(part.astype(BF16))
        line = jnp.concatenate(parts, axis=1)
        masked[rows, :] = line

    @pl.when(yl == 0)
    def _():
        keep[...] = masked[:, :HALF]
        away[...] = masked[:, HALF:]

    @pl.when(yl == 1)
    def _():
        keep[...] = masked[:, HALF:]
        away[...] = masked[:, :HALF]


def tiles(body):
    row, col = lax.axis_index("row"), lax.axis_index("col")
    for i in range(ROWS // SLAB):
        for j in range(COLS // BLOCK):
            rows, cols = slice(SLAB * i, SLAB * (i + 1)), slice(BLOCK * j, BLOCK * (j + 1))
            body(rows, cols, (row * 3 + i) // 2, col * 6 + j)


def fill_ring(put, pieces):
    own, other, a1, b1, a2, b2, a3, b3, a4, *far = pieces
    z, _, core, _ = place()
    sign, rows = 2 * core - 1, own.shape[0]

    def place_piece(ref, start, k, which):
        put(ref, start * rows, lax.rem(k + 16, 8), which)

    place_piece(own, 0, z, core)
    place_piece(other, 0, z, 1 - core)
    for s, (a, b) in enumerate(((a1, b1), (a2, b2), (a3, b3))):
        place_piece(a, 0, z + sign * (s + 1), core)
        place_piece(b, 0, z + sign * (s + 1), 1 - core)
        place_piece(far[s], 0, z - sign * (s + 1), 1 - core)
        place_piece(far[s], 1, z - sign * (s + 1), core)
    place_piece(a4, 0, z + 4, core)
    place_piece(far[3], 0, z + 4, 1 - core)


def fill_left(left, pieces):
    own, w, e, y, x2, x2_too, yw, ye, y2 = pieces
    _, _, _, col = place()
    yh, x = col // 4, col % 4

    def at(dx, dy):
        return lax.rem(yh + dy, 2) * 4 + lax.rem(x + dx + 4, 4)

    left[at(0, 0)] = own[...]
    left[at(-1, 0)] = w[...]
    left[at(1, 0)] = e[...]
    left[at(0, 1)] = y[...]
    left[at(2, 0), :ROWS, :] = x2[...]
    left[at(2, 0), ROWS:, :] = x2_too[...]
    left[at(-1, 1)] = yw[...]
    left[at(1, 1)] = ye[...]
    left[at(2, 1)] = y2[...]


def multiply(left, column, kept, away):
    def part(k):
        return jnp.dot(left[k], column[k].reshape(HALF, COLS), preferred_element_type=F32)

    total = sum((part(k) for k in range(1, 8)), part(0))
    kept[...] = total[:ROWS]
    away[...] = total[ROWS:].astype(BF16)


def fill_column(column, pieces):
    def put(ref, start, k, which):
        column[k, which] = ref[start : start + ROWS, :]

    fill_ring(put, pieces)


def square_kernel(*refs):
    kept, away, left, column = refs[22:]
    fill_left(left, refs[:9])
    fill_column(column, refs[9:22])
    multiply(left, column, kept, away)


def update_kernel(*refs):
    kept, away, column = refs[14:]
    fill_column(column, refs[1:14])
    multiply(refs[0], column, kept, away)


def weight_kernel(keep, kept, theirs, weight):
    row, col = lax.axis_index("row"), lax.axis_index("col")

    def body(rows, cols, a, b):
        factor = jnp.where(listed(keep, a, b), 0.5, 0.0).astype(F32)
        down = lax.broadcasted_iota(jnp.int32, (SLAB, BLOCK), 0) + (row * ROWS + rows.start)
        over = lax.broadcasted_iota(jnp.int32, (SLAB, BLOCK), 1) + (col * COLS + cols.start)
        eye = jnp.where(down == over, 1.5, 0.0).astype(F32)
        square = kept[rows, cols] + theirs[rows, cols].astype(F32)
        weight[rows, cols] = (eye - square * factor).astype(BF16)

    tiles(body)


def result_kernel(pattern, kept, theirs, result):
    def body(rows, cols, a, b):
        factor = jnp.where(listed(pattern, a, b) | (a == b), 1.0, 0.0).astype(F32)
        total = kept[rows, cols] + theirs[rows, cols].astype(F32)
        result[rows, cols] = (total * factor).astype(BF16)

    tiles(body)


SMEM, VMEM = (pl.BlockSpec(memory_space=space) for space in (pltpu.SMEM, pltpu.VMEM))


def struct(*shape, dtype=BF16):
    return jax.ShapeDtypeStruct(shape, dtype)


def call(kernel, args, outs, scratch, flops):
    return pl.pallas_call(
        kernel,
        in_specs=[SMEM if arg.dtype == jnp.int32 else VMEM for arg in args],
        out_specs=[VMEM] * len(outs),
        out_shape=outs,
        scratch_shapes=scratch,
        cost_estimate=pl.CostEstimate(flops=flops, bytes_accessed=0, transcendentals=0),
        compiler_params=pltpu.CompilerParams(vmem_limit_bytes=VMEM_LIMIT),
    )(*args)


def after(value, *others):
    return lax.optimization_barrier((value, *others))[0]


def ring(piece, first=(), second=(), third=(), fourth=(), last=()):
    other = send(piece, CORE)
    a1, b1 = send(piece, RING), send(other, RING)
    a2, b2 = send(after(a1, *first), RING), send(b1, RING)
    a3, b3 = send(after(a2, *second), RING), send(after(b2, *third), RING)
    a4 = send(after(a3, *fourth), RING)
    far = [send(cat(a, b), CORE) for a, b in ((a1, b1), (a2, b2), (a3, b3))]
    return [piece, other, a1, b1, a2, b2, a3, b3, a4, *far, send(after(a4, *last), CORE)]


def row(piece):
    w, e, y = send(piece, EAST), send(piece, WEST), send(piece, ACROSS)
    x2, x2_too = send(w[:ROWS], EAST), send(e[ROWS:], WEST)
    yw, ye = send(y, EAST), send(y, WEST)
    y2 = send(cat(x2, x2_too), ACROSS)
    return [piece, w, e, y, x2, x2_too, yw, ye, y2]


FLOPS = 2 * ROWS * COLS * 6144
SUMS = [struct(ROWS, COLS, dtype=F32), struct(ROWS, COLS)]
COLUMN = pltpu.VMEM((8, 2, ROWS, COLS), BF16)


def shards(matrix, pattern, keep):
    x, kept, away = call(
        mask_kernel,
        [pattern, matrix],
        [struct(ROWS, COLS), struct(ROWS, HALF), struct(ROWS, HALF)],
        [],
        0,
    )
    pieces = row(cat(kept, send(away, TWIN)))
    kept, away, left = call(
        square_kernel,
        [*pieces, *ring(x, pieces[:1], pieces[1:4], pieces[4:6], pieces[6:8], pieces[8:])],
        [*SUMS, struct(8, HALF, HALF)],
        [COLUMN],
        FLOPS,
    )
    (weight,) = call(weight_kernel, [keep, kept, send(away, TWIN)], [struct(ROWS, COLS)], [], 0)
    kept, away = call(update_kernel, [left, *ring(weight)], SUMS, [COLUMN], FLOPS)
    (result,) = call(result_kernel, [pattern, kept, send(away, TWIN)], [struct(ROWS, COLS)], [], 0)
    return result


def solution(mesh):
    return jax.shard_map(
        shards,
        mesh=mesh,
        in_specs=(P("row", "col"), P(), P()),
        out_specs=P("row", "col"),
        check_vma=False,
    )
```

```python
import functools

import jax
import jax.numpy as jnp
import numpy as np
from jax import lax
from jax.experimental import pallas as pl
from jax.experimental.pallas import tpu as pltpu
from jax.sharding import PartitionSpec as P

SIZES = (8, 2, 2, 2, 4)
AXES = ("row", "col")
ROWS, COLS = 192, 768
HALF = COLS // 2
SLAB, BLOCK = 64, 128
VMEM_LIMIT = 18 * 1024 * 1024
F32, BF16 = jnp.float32, jnp.bfloat16


def moves(step):
    pairs = []
    for index, place in enumerate(np.ndindex(*SIZES)):
        target = np.mod(step(*place), SIZES)
        pairs.append((index, int(np.ravel_multi_index(target, SIZES))))
    return pairs


def along_y(sign):
    def step(z, yl, core, yh, x):
        y = (2 * yh + yl + sign) % 4
        return z, y % 2, core, y // 2, x

    return moves(step)


EAST = moves(lambda z, yl, core, yh, x: (z, yl, core, yh, x + 1))
WEST = moves(lambda z, yl, core, yh, x: (z, yl, core, yh, x - 1))
NORTH, SOUTH = along_y(1), along_y(-1)
ACROSS = moves(lambda z, yl, core, yh, x: (z, yl, core, 1 - yh, x))
TWIN = moves(lambda z, yl, core, yh, x: (z, 1 - yl, core, yh, x))
CORE = moves(lambda z, yl, core, yh, x: (z, yl, 1 - core, yh, x))
RING = moves(lambda z, yl, core, yh, x: (z + 1 - 2 * core, yl, core, yh, x))


def send(value, pairs):
    return lax.ppermute(value, AXES, pairs)


def cat(*parts):
    return jnp.concatenate(parts, axis=0)


def place():
    row, col = lax.axis_index("row"), lax.axis_index("col")
    return row // 4, (row // 2) % 2, row % 2, col


def listed(table, a, b):
    return table[jnp.minimum(a, b), jnp.maximum(a, b)] > 0


def mask_kernel(pattern, matrix, masked, keep, away, table, block, sems):
    fetches = [
        pltpu.make_async_copy(pattern, table, sems.at[0]),
        pltpu.make_async_copy(matrix, block, sems.at[1]),
    ]
    for fetch in fetches:
        fetch.start()
    for fetch in fetches:
        fetch.wait()
    _, yl, _, _ = place()

    def body(rows, cols, a, b):
        factor = jnp.where(listed(table, a, b) | (a == b), 1.0, 0.0).astype(F32)
        masked[rows, cols] = (block[rows, cols].astype(F32) * factor).astype(BF16)

    tiles(body)

    @pl.when(yl == 0)
    def _():
        keep[...] = masked[:, :HALF]
        away[...] = masked[:, HALF:]

    @pl.when(yl == 1)
    def _():
        keep[...] = masked[:, HALF:]
        away[...] = masked[:, :HALF]


def tiles(body):
    row, col = lax.axis_index("row"), lax.axis_index("col")
    for i in range(ROWS // SLAB):
        for j in range(COLS // BLOCK):
            rows, cols = slice(SLAB * i, SLAB * (i + 1)), slice(BLOCK * j, BLOCK * (j + 1))
            body(rows, cols, (row * 3 + i) // 2, col * 6 + j)


def fill_left(left, pieces):
    own, w, e, y, x2, x2_too, yw, ye, y2 = pieces
    _, _, _, col = place()
    yh, x = col // 4, col % 4

    def at(dx, dy):
        return lax.rem(yh + dy, 2) * 4 + lax.rem(x + dx + 4, 4)

    left[at(0, 0)] = own[...]
    left[at(-1, 0)] = w[...]
    left[at(1, 0)] = e[...]
    left[at(0, 1)] = y[...]
    left[at(2, 0), :ROWS, :] = x2[...]
    left[at(2, 0), ROWS:, :] = x2_too[...]
    left[at(-1, 1)] = yw[...]
    left[at(1, 1)] = ye[...]
    left[at(2, 1)] = y2[...]


def multiply(left, rows, blocks):
    _, _, core, _ = place()

    def part(k, mine, others, pair):
        pair[core] = mine[...]
        pair[1 - core] = others[...]
        right = pair[...].reshape(HALF, COLS)
        return jnp.dot(left[lax.rem(k + 16, 8), rows], right, preferred_element_type=F32)

    return sum((part(*block) for block in blocks[1:]), part(*blocks[0]))


def near_sums(left, pieces, column):
    z, _, core, _ = place()
    sign = 2 * core - 1
    pairs = [(pieces[2 * s], pieces[2 * s + 1], column.at[s]) for s in range(4)]
    return multiply(left, slice(0, HALF), [(z + sign * s, *pair) for s, pair in enumerate(pairs)])


def square_kernel(*refs):
    total, left, column = refs[17:]
    fill_left(left, refs[:9])
    total[...] = near_sums(left, refs[9:17], column)


def update_kernel(*refs):
    total, column = refs[9:]
    total[...] = near_sums(refs[0], refs[1:9], column)


def last_kernel(part, left, total, a4, s1, s2, s3, s4, result, column):
    z, _, core, _ = place()
    sign = 2 * core - 1
    rows = slice(ROWS * part, ROWS * (part + 1))
    blocks = [(z + 4, a4, s4, column.at[3])]
    for s, ref in enumerate((s1, s2, s3)):
        blocks.append((z - sign * (s + 1), ref.at[ROWS:], ref.at[:ROWS], column.at[s]))
    result[...] = (total[rows] + multiply(left, rows, blocks)).astype(result.dtype)


def factor_kernel(pattern, keep, kept_square, eye, kept_result):
    row, col = lax.axis_index("row"), lax.axis_index("col")

    def body(rows, cols, a, b):
        shape = (SLAB, BLOCK)
        down = lax.broadcasted_iota(jnp.int32, shape, 0) + (row * ROWS + rows.start)
        over = lax.broadcasted_iota(jnp.int32, shape, 1) + (col * COLS + cols.start)
        eye[rows, cols] = jnp.where(down == over, 1.5, 0.0).astype(F32)
        square_factor = jnp.where(listed(keep, a, b), 0.5, 0.0).astype(F32)
        kept_square[rows, cols] = jnp.full(shape, square_factor, F32)
        result_factor = jnp.where(listed(pattern, a, b) | (a == b), 1.0, 0.0).astype(F32)
        kept_result[rows, cols] = jnp.full(shape, result_factor, F32)

    tiles(body)


SMEM, VMEM = (pl.BlockSpec(memory_space=space) for space in (pltpu.SMEM, pltpu.VMEM))


def struct(*shape, dtype=BF16):
    return jax.ShapeDtypeStruct(shape, dtype)


def call(kernel, args, outs, scratch, flops, specs=None):
    return pl.pallas_call(
        kernel,
        in_specs=specs or [SMEM if arg.dtype == jnp.int32 else VMEM for arg in args],
        out_specs=[VMEM] * len(outs),
        out_shape=outs,
        scratch_shapes=scratch,
        cost_estimate=pl.CostEstimate(flops=flops, bytes_accessed=0, transcendentals=0),
        compiler_params=pltpu.CompilerParams(vmem_limit_bytes=VMEM_LIMIT),
    )(*args)


def after(value, *others):
    return lax.optimization_barrier((value, *others))[0]


def ring(piece, multiply_by, **awaited):
    def step(value, name):
        return send(after(value, *awaited.get(name, ())), RING)

    other = send(piece, CORE)
    a1, b1 = step(piece, "a1"), step(other, "b1")
    a2, b2 = step(a1, "a2"), step(b1, "b2")
    a3, b3 = step(a2, "a3"), step(b2, "b3")
    a4 = step(a3, "a4")
    sums = multiply_by([piece, other, a1, b1, a2, b2, a3, b3])
    far = [send(cat(a, b), CORE) for a, b in ((a1, b1), (a2, b2), (a3, b3))]
    return sums, [a4, *far, send(after(a4, sums[0]), CORE)]


def row(piece):
    w, e, y = send(piece, EAST), send(piece, WEST), send(piece, ACROSS)
    x2, x2_too = send(w[:ROWS], EAST), send(e[ROWS:], WEST)
    yw, ye = send(y, EAST), send(y, WEST)
    y2 = send(cat(x2, x2_too), ACROSS)
    return [piece, w, e, y, x2, x2_too, yw, ye, y2]


FLOPS = 2 * ROWS * COLS * 6144
SUMS = struct(HALF, COLS, dtype=F32)
COLUMN = pltpu.VMEM((4, 2, ROWS, COLS), BF16)


def sums(left, total, last):
    args = [left, total, *last]
    away_kernel, keep_kernel = functools.partial(last_kernel, 1), functools.partial(last_kernel, 0)
    (away,) = call(away_kernel, args, [struct(ROWS, COLS)], [COLUMN], FLOPS // 4)
    theirs = send(away, TWIN)
    (kept,) = call(keep_kernel, args, [struct(ROWS, COLS, dtype=F32)], [COLUMN], FLOPS // 4)
    return kept + theirs.astype(F32)


def shards(matrix, pattern, keep):
    x, kept, away = call(
        mask_kernel,
        [pattern, matrix],
        [struct(ROWS, COLS), struct(ROWS, HALF), struct(ROWS, HALF)],
        [pltpu.SMEM((48, 48), jnp.int32), pltpu.VMEM((ROWS, COLS), BF16), pltpu.SemaphoreType.DMA((2,))],
        0,
        [pl.BlockSpec(memory_space=pltpu.HBM)] * 2,
    )
    kept_square, eye, kept_result = call(
        factor_kernel, [pattern, keep], [struct(ROWS, COLS, dtype=F32)] * 3, [], ROWS * COLS
    )
    pieces = row(cat(kept, send(away, TWIN)))

    def square(near):
        return call(square_kernel, [*pieces, *near], [SUMS, struct(8, HALF, HALF)], [COLUMN], FLOPS // 2)

    (total, left), last = ring(x, square, a2=pieces[:1], a3=pieces[1:4], b3=pieces[4:6], a4=pieces[6:8])
    weight = (eye - sums(left, total, last) * kept_square).astype(BF16)

    def update(near):
        return call(update_kernel, [left, *near], [SUMS], [COLUMN], FLOPS // 2)

    (total,), last = ring(weight, update)
    return (sums(left, total, last) * kept_result).astype(BF16)


def solution(mesh):
    return jax.shard_map(
        shards,
        mesh=mesh,
        in_specs=(P("row", "col"), P(), P()),
        out_specs=P("row", "col"),
        check_vma=False,
    )
```

```python
import functools

import jax
import jax.numpy as jnp
import numpy as np
from jax import lax
from jax.experimental import pallas as pl
from jax.experimental.pallas import tpu as pltpu
from jax.sharding import PartitionSpec as P

SIZES = (8, 2, 2, 2, 4)
AXES = ("row", "col")
ROWS, COLS = 192, 768
HALF = COLS // 2
SLAB, BLOCK = 64, 128
VMEM_LIMIT = 18 * 1024 * 1024
F32, BF16 = jnp.float32, jnp.bfloat16


def moves(step):
    pairs = []
    for index, place in enumerate(np.ndindex(*SIZES)):
        target = np.mod(step(*place), SIZES)
        pairs.append((index, int(np.ravel_multi_index(target, SIZES))))
    return pairs


def along_y(sign):
    def step(z, yl, core, yh, x):
        y = (2 * yh + yl + sign) % 4
        return z, y % 2, core, y // 2, x

    return moves(step)


EAST = moves(lambda z, yl, core, yh, x: (z, yl, core, yh, x + 1))
WEST = moves(lambda z, yl, core, yh, x: (z, yl, core, yh, x - 1))
NORTH, SOUTH = along_y(1), along_y(-1)
ACROSS = moves(lambda z, yl, core, yh, x: (z, yl, core, 1 - yh, x))
TWIN = moves(lambda z, yl, core, yh, x: (z, 1 - yl, core, yh, x))
CORE = moves(lambda z, yl, core, yh, x: (z, yl, 1 - core, yh, x))
RING = moves(lambda z, yl, core, yh, x: (z + 1 - 2 * core, yl, core, yh, x))


def send(value, pairs):
    return lax.ppermute(value, AXES, pairs)


def cat(*parts):
    return jnp.concatenate(parts, axis=0)


def place():
    row, col = lax.axis_index("row"), lax.axis_index("col")
    return row // 4, (row // 2) % 2, row % 2, col


def listed(table, a, b):
    return table[jnp.minimum(a, b), jnp.maximum(a, b)] > 0


def mask_kernel(pattern, matrix, masked, keep, away, table, block, sems):
    fetches = [
        pltpu.make_async_copy(pattern, table, sems.at[0]),
        pltpu.make_async_copy(matrix, block, sems.at[1]),
    ]
    for fetch in fetches:
        fetch.start()
    for fetch in fetches:
        fetch.wait()
    _, yl, _, _ = place()

    def body(rows, cols, a, b):
        factor = jnp.where(listed(table, a, b) | (a == b), 1.0, 0.0).astype(F32)
        masked[rows, cols] = (block[rows, cols].astype(F32) * factor).astype(BF16)

    tiles(body)

    @pl.when(yl == 0)
    def _():
        keep[...] = masked[:, :HALF]
        away[...] = masked[:, HALF:]

    @pl.when(yl == 1)
    def _():
        keep[...] = masked[:, HALF:]
        away[...] = masked[:, :HALF]


def tiles(body):
    row, col = lax.axis_index("row"), lax.axis_index("col")
    for i in range(ROWS // SLAB):
        for j in range(COLS // BLOCK):
            rows, cols = slice(SLAB * i, SLAB * (i + 1)), slice(BLOCK * j, BLOCK * (j + 1))
            body(rows, cols, (row * 3 + i) // 2, col * 6 + j)


def fill_left(left, pieces):
    own, w, e, y, x2, x2_too, yw, ye, y2 = pieces
    _, _, _, col = place()
    yh, x = col // 4, col % 4

    def at(dx, dy):
        return lax.rem(yh + dy, 2) * 4 + lax.rem(x + dx + 4, 4)

    left[at(0, 0)] = own[...]
    left[at(-1, 0)] = w[...]
    left[at(1, 0)] = e[...]
    left[at(0, 1)] = y[...]
    left[at(2, 0), :ROWS, :] = x2[...]
    left[at(2, 0), ROWS:, :] = x2_too[...]
    left[at(-1, 1)] = yw[...]
    left[at(1, 1)] = ye[...]
    left[at(2, 1)] = y2[...]


def multiply(left, rows, blocks):
    _, _, core, _ = place()

    def part(k, mine, others, pair):
        pair[core] = mine[...]
        pair[1 - core] = others[...]
        right = pair[...].reshape(HALF, COLS)
        return jnp.dot(left[lax.rem(k + 16, 8), rows], right, preferred_element_type=F32)

    return sum((part(*block) for block in blocks[1:]), part(*blocks[0]))


def near_sums(left, pieces, column):
    z, _, core, _ = place()
    sign = 2 * core - 1
    pairs = [(pieces[2 * s], pieces[2 * s + 1], column.at[s]) for s in range(4)]
    return multiply(left, slice(0, HALF), [(z + sign * s, *pair) for s, pair in enumerate(pairs)])


def square_kernel(*refs):
    total, left, column = refs[17:]
    fill_left(left, refs[:9])
    total[...] = near_sums(left, refs[9:17], column)


def update_kernel(*refs):
    total, column = refs[9:]
    total[...] = near_sums(refs[0], refs[1:9], column)


def last_kernel(part, left, total, a4, s1, s2, s3, s4, result, column):
    z, _, core, _ = place()
    sign = 2 * core - 1
    rows = slice(ROWS * part, ROWS * (part + 1))
    blocks = [(z + 4, a4, s4, column.at[3])]
    for s, ref in enumerate((s1, s2, s3)):
        blocks.append((z - sign * (s + 1), ref.at[ROWS:], ref.at[:ROWS], column.at[s]))
    result[...] = (total[rows] + multiply(left, rows, blocks)).astype(result.dtype)


def factor_kernel(pattern, keep, kept_square, eye, kept_result):
    row, col = lax.axis_index("row"), lax.axis_index("col")

    def body(rows, cols, a, b):
        shape = (SLAB, BLOCK)
        down = lax.broadcasted_iota(jnp.int32, shape, 0) + (row * ROWS + rows.start)
        over = lax.broadcasted_iota(jnp.int32, shape, 1) + (col * COLS + cols.start)
        eye[rows, cols] = jnp.where(down == over, 1.5, 0.0).astype(F32)
        square_factor = jnp.where(listed(keep, a, b), 0.5, 0.0).astype(F32)
        kept_square[rows, cols] = jnp.full(shape, square_factor, F32)
        result_factor = jnp.where(listed(pattern, a, b) | (a == b), 1.0, 0.0).astype(F32)
        kept_result[rows, cols] = jnp.full(shape, result_factor, F32)

    tiles(body)


SMEM, VMEM = (pl.BlockSpec(memory_space=space) for space in (pltpu.SMEM, pltpu.VMEM))


def struct(*shape, dtype=BF16):
    return jax.ShapeDtypeStruct(shape, dtype)


def call(kernel, args, outs, scratch, flops, specs=None):
    return pl.pallas_call(
        kernel,
        in_specs=specs or [SMEM if arg.dtype == jnp.int32 else VMEM for arg in args],
        out_specs=[VMEM] * len(outs),
        out_shape=outs,
        scratch_shapes=scratch,
        cost_estimate=pl.CostEstimate(flops=flops, bytes_accessed=0, transcendentals=0),
        compiler_params=pltpu.CompilerParams(vmem_limit_bytes=VMEM_LIMIT),
    )(*args)


def after(value, *others):
    return lax.optimization_barrier((value, *others))[0]


def ring(piece, multiply_by, **awaited):
    def step(value, name):
        return send(after(value, *awaited.get(name, ())), RING)

    other = send(piece, CORE)
    a1, b1 = step(piece, "a1"), step(other, "b1")
    a2, b2 = step(a1, "a2"), step(b1, "b2")
    a3, b3 = step(a2, "a3"), step(b2, "b3")
    a4 = step(a3, "a4")
    sums = multiply_by([piece, other, a1, b1, a2, b2, a3, b3])
    far = [send(cat(a, b), CORE) for a, b in ((a1, b1), (a2, b2), (a3, b3))]
    return sums, [a4, *far, send(after(a4, sums[0]), CORE)]


def row(piece):
    w, e, y = send(piece, EAST), send(piece, WEST), send(piece, ACROSS)
    x2, x2_too = send(w[:ROWS], EAST), send(e[ROWS:], WEST)
    yw, ye = send(y, EAST), send(y, WEST)
    y2 = send(cat(x2, x2_too), ACROSS)
    return [piece, w, e, y, x2, x2_too, yw, ye, y2]


FLOPS = 2 * ROWS * COLS * 6144
SUMS = struct(HALF, COLS, dtype=F32)
COLUMN = pltpu.VMEM((4, 2, ROWS, COLS), BF16)


def sums(left, total, last):
    args = [left, total, *last]
    away_kernel, keep_kernel = functools.partial(last_kernel, 1), functools.partial(last_kernel, 0)
    (away,) = call(away_kernel, args, [struct(ROWS, COLS)], [COLUMN], FLOPS // 4)
    theirs = send(away, TWIN)
    (kept,) = call(keep_kernel, args, [struct(ROWS, COLS, dtype=F32)], [COLUMN], FLOPS // 4)
    return kept + theirs.astype(F32)


def in_hbm(value):
    return pltpu.with_memory_space_constraint(value, pltpu.HBM)


def shards(matrix, pattern, keep):
    x, kept, away = call(
        mask_kernel,
        [in_hbm(pattern), in_hbm(matrix)],
        [struct(ROWS, COLS), struct(ROWS, HALF), struct(ROWS, HALF)],
        [pltpu.SMEM((48, 48), jnp.int32), pltpu.VMEM((ROWS, COLS), BF16), pltpu.SemaphoreType.DMA((2,))],
        0,
        [pl.BlockSpec(memory_space=pltpu.HBM)] * 2,
    )
    kept_square, eye, kept_result = call(
        factor_kernel, [pattern, keep], [struct(ROWS, COLS, dtype=F32)] * 3, [], ROWS * COLS
    )
    pieces = row(cat(kept, send(away, TWIN)))

    def square(near):
        return call(square_kernel, [*pieces, *near], [SUMS, struct(8, HALF, HALF)], [COLUMN], FLOPS // 2)

    (total, left), last = ring(x, square, a2=pieces[:1], a3=pieces[1:4], b3=pieces[4:6], a4=pieces[6:8])
    weight = (eye - sums(left, total, last) * kept_square).astype(BF16)

    def update(near):
        return call(update_kernel, [left, *near], [SUMS], [COLUMN], FLOPS // 2)

    (total,), last = ring(weight, update)
    return (sums(left, total, last) * kept_result).astype(BF16)


def solution(mesh):
    return jax.shard_map(
        shards,
        mesh=mesh,
        in_specs=(P("row", "col"), P(), P()),
        out_specs=P("row", "col"),
        check_vma=False,
    )
```

```python
import functools

import jax
import jax.numpy as jnp
import numpy as np
from jax import lax
from jax.experimental import pallas as pl
from jax.experimental.pallas import tpu as pltpu
from jax.sharding import PartitionSpec as P

SIZES = (8, 2, 2, 2, 4)
AXES = ("row", "col")
ROWS, COLS = 192, 768
HALF = COLS // 2
SLAB, BLOCK = 64, 128
VMEM_LIMIT = 18 * 1024 * 1024
F32, BF16 = jnp.float32, jnp.bfloat16


def moves(step):
    pairs = []
    for index, place in enumerate(np.ndindex(*SIZES)):
        target = np.mod(step(*place), SIZES)
        pairs.append((index, int(np.ravel_multi_index(target, SIZES))))
    return pairs


def along_y(sign):
    def step(z, yl, core, yh, x):
        y = (2 * yh + yl + sign) % 4
        return z, y % 2, core, y // 2, x

    return moves(step)


EAST = moves(lambda z, yl, core, yh, x: (z, yl, core, yh, x + 1))
WEST = moves(lambda z, yl, core, yh, x: (z, yl, core, yh, x - 1))
NORTH, SOUTH = along_y(1), along_y(-1)
ACROSS = moves(lambda z, yl, core, yh, x: (z, yl, core, 1 - yh, x))
TWIN = moves(lambda z, yl, core, yh, x: (z, 1 - yl, core, yh, x))
CORE = moves(lambda z, yl, core, yh, x: (z, yl, 1 - core, yh, x))
RING = moves(lambda z, yl, core, yh, x: (z + 1 - 2 * core, yl, core, yh, x))


def send(value, pairs):
    return lax.ppermute(value, AXES, pairs)


def cat(*parts):
    return jnp.concatenate(parts, axis=0)


def place():
    row, col = lax.axis_index("row"), lax.axis_index("col")
    return row // 4, (row // 2) % 2, row % 2, col


def listed(table, a, b):
    return table[jnp.minimum(a, b), jnp.maximum(a, b)] > 0


def mask_kernel(pattern, matrix, masked, keep, away, table, block, sems):
    fetches = [
        pltpu.make_async_copy(pattern, table, sems.at[0]),
        pltpu.make_async_copy(matrix, block, sems.at[1]),
    ]
    for fetch in fetches:
        fetch.start()
    for fetch in fetches:
        fetch.wait()
    _, yl, _, _ = place()

    def body(rows, cols, a, b):
        factor = jnp.where(listed(table, a, b) | (a == b), 1.0, 0.0).astype(F32)
        masked[rows, cols] = (block[rows, cols].astype(F32) * factor).astype(BF16)

    tiles(body)

    @pl.when(yl == 0)
    def _():
        keep[...] = masked[:, :HALF]
        away[...] = masked[:, HALF:]

    @pl.when(yl == 1)
    def _():
        keep[...] = masked[:, HALF:]
        away[...] = masked[:, :HALF]


def tiles(body):
    row, col = lax.axis_index("row"), lax.axis_index("col")
    for i in range(ROWS // SLAB):
        for j in range(COLS // BLOCK):
            rows, cols = slice(SLAB * i, SLAB * (i + 1)), slice(BLOCK * j, BLOCK * (j + 1))
            body(rows, cols, (row * 3 + i) // 2, col * 6 + j)


def fill_left(left, pieces):
    own, w, e, y, x2, x2_too, yw, ye, y2 = pieces
    _, _, _, col = place()
    yh, x = col // 4, col % 4

    def put(ref, dx, dy, first=0):
        index = lax.rem(yh + dy, 2) * 4 + lax.rem(x + dx + 4, 4)
        for core in range(2):
            columns = slice(ROWS * core, ROWS * (core + 1))
            left[index, core, first : first + ref.shape[0], :] = ref[:, columns]

    put(own, 0, 0)
    put(w, -1, 0)
    put(e, 1, 0)
    put(y, 0, 1)
    put(x2, 2, 0)
    put(x2_too, 2, 0, ROWS)
    put(yw, -1, 1)
    put(ye, 1, 1)
    put(y2, 2, 1)


def multiply(left, rows, parts):
    def part(k, core, ref, first):
        return jnp.dot(
            left[lax.rem(k + 16, 8), core, rows], ref[first : first + ROWS, :], preferred_element_type=F32
        )

    return sum((part(*p) for p in parts[1:]), part(*parts[0]))


def near_sums(left, pieces):
    z, _, core, _ = place()
    sign = 2 * core - 1
    parts = []
    for s in range(4):
        parts.append((z + sign * s, core, pieces[2 * s], 0))
        parts.append((z + sign * s, 1 - core, pieces[2 * s + 1], 0))
    return multiply(left, slice(0, HALF), parts)


def square_kernel(*refs):
    total, left = refs[17:]
    fill_left(left, refs[:9])
    total[...] = near_sums(left, refs[9:17])


def update_kernel(*refs):
    refs[9][...] = near_sums(refs[0], refs[1:9])


def last_kernel(half, left, total, a4, s1, s2, s3, s4, result):
    z, _, core, _ = place()
    sign = 2 * core - 1
    rows = slice(ROWS * half, ROWS * (half + 1))
    parts = [(z + 4, core, a4, 0), (z + 4, 1 - core, s4, 0)]
    for s, ref in enumerate((s1, s2, s3)):
        parts.append((z - sign * (s + 1), 1 - core, ref, 0))
        parts.append((z - sign * (s + 1), core, ref, ROWS))
    result[...] = (total[rows] + multiply(left, rows, parts)).astype(result.dtype)


def factor_kernel(pattern, keep, kept_square, eye, kept_result):
    row, col = lax.axis_index("row"), lax.axis_index("col")

    def body(rows, cols, a, b):
        shape = (SLAB, BLOCK)
        down = lax.broadcasted_iota(jnp.int32, shape, 0) + (row * ROWS + rows.start)
        over = lax.broadcasted_iota(jnp.int32, shape, 1) + (col * COLS + cols.start)
        eye[rows, cols] = jnp.where(down == over, 1.5, 0.0).astype(F32)
        square_factor = jnp.where(listed(keep, a, b), 0.5, 0.0).astype(F32)
        kept_square[rows, cols] = jnp.full(shape, square_factor, F32)
        result_factor = jnp.where(listed(pattern, a, b) | (a == b), 1.0, 0.0).astype(F32)
        kept_result[rows, cols] = jnp.full(shape, result_factor, F32)

    tiles(body)


SMEM, VMEM = (pl.BlockSpec(memory_space=space) for space in (pltpu.SMEM, pltpu.VMEM))


def struct(*shape, dtype=BF16):
    return jax.ShapeDtypeStruct(shape, dtype)


def call(kernel, args, outs, scratch, flops, specs=None):
    return pl.pallas_call(
        kernel,
        in_specs=specs or [SMEM if arg.dtype == jnp.int32 else VMEM for arg in args],
        out_specs=[VMEM] * len(outs),
        out_shape=outs,
        scratch_shapes=scratch,
        cost_estimate=pl.CostEstimate(flops=flops, bytes_accessed=0, transcendentals=0),
        compiler_params=pltpu.CompilerParams(vmem_limit_bytes=VMEM_LIMIT),
    )(*args)


def after(value, *others):
    return lax.optimization_barrier((value, *others))[0]


def ring(piece, multiply_by, **awaited):
    def step(value, name):
        return send(after(value, *awaited.get(name, ())), RING)

    other = send(piece, CORE)
    a1, b1 = step(piece, "a1"), step(other, "b1")
    a2, b2 = step(a1, "a2"), step(b1, "b2")
    a3, b3 = step(a2, "a3"), step(b2, "b3")
    a4 = step(a3, "a4")
    sums = multiply_by([piece, other, a1, b1, a2, b2, a3, b3])
    far = [send(cat(a, b), CORE) for a, b in ((a1, b1), (a2, b2), (a3, b3))]
    return sums, [a4, *far, send(after(a4, sums[0]), CORE)]


def row(piece):
    w, e, y = send(piece, EAST), send(piece, WEST), send(piece, ACROSS)
    x2, x2_too = send(w[:ROWS], EAST), send(e[ROWS:], WEST)
    yw, ye = send(y, EAST), send(y, WEST)
    y2 = send(cat(x2, x2_too), ACROSS)
    return [piece, w, e, y, x2, x2_too, yw, ye, y2]


FLOPS = 2 * ROWS * COLS * 6144
SUMS = struct(HALF, COLS, dtype=F32)


def sums(left, total, last):
    args = [left, total, *last]
    away_kernel, keep_kernel = functools.partial(last_kernel, 1), functools.partial(last_kernel, 0)
    (away,) = call(away_kernel, args, [struct(ROWS, COLS)], [], FLOPS // 4)
    theirs = send(away, TWIN)
    (kept,) = call(keep_kernel, args, [struct(ROWS, COLS, dtype=F32)], [], FLOPS // 4)
    return kept + theirs.astype(F32)


def in_hbm(value):
    return pltpu.with_memory_space_constraint(value, pltpu.HBM)


def shards(matrix, pattern, keep):
    x, kept, away = call(
        mask_kernel,
        [in_hbm(pattern), in_hbm(matrix)],
        [struct(ROWS, COLS), struct(ROWS, HALF), struct(ROWS, HALF)],
        [pltpu.SMEM((48, 48), jnp.int32), pltpu.VMEM((ROWS, COLS), BF16), pltpu.SemaphoreType.DMA((2,))],
        0,
        [pl.BlockSpec(memory_space=pltpu.HBM)] * 2,
    )
    kept_square, eye, kept_result = call(
        factor_kernel, [pattern, keep], [struct(ROWS, COLS, dtype=F32)] * 3, [], ROWS * COLS
    )
    pieces = row(cat(kept, send(away, TWIN)))

    def square(near):
        return call(square_kernel, [*pieces, *near], [SUMS, struct(8, 2, HALF, ROWS)], [], FLOPS // 2)

    (total, left), last = ring(x, square, a2=pieces[:1], a3=pieces[1:4], b3=pieces[4:6], a4=pieces[6:8])
    weight = (eye - sums(left, total, last) * kept_square).astype(BF16)

    def update(near):
        return call(update_kernel, [left, *near], [SUMS], [], FLOPS // 2)

    (total,), last = ring(weight, update)
    return (sums(left, total, last) * kept_result).astype(BF16)


def solution(mesh):
    return jax.shard_map(
        shards,
        mesh=mesh,
        in_specs=(P("row", "col"), P(), P()),
        out_specs=P("row", "col"),
        check_vma=False,
    )
```

```python
import functools

import jax
import jax.numpy as jnp
import numpy as np
from jax import lax
from jax.experimental import pallas as pl
from jax.experimental.pallas import tpu as pltpu
from jax.sharding import PartitionSpec as P

SIZES = (8, 2, 2, 2, 4)
AXES = ("row", "col")
ROWS, COLS = 192, 768
HALF = COLS // 2
SLAB, BLOCK = 64, 128
VMEM_LIMIT = 18 * 1024 * 1024
F32, BF16 = jnp.float32, jnp.bfloat16


def moves(step):
    pairs = []
    for index, place in enumerate(np.ndindex(*SIZES)):
        target = np.mod(step(*place), SIZES)
        pairs.append((index, int(np.ravel_multi_index(target, SIZES))))
    return pairs


def along_y(sign):
    def step(z, yl, core, yh, x):
        y = (2 * yh + yl + sign) % 4
        return z, y % 2, core, y // 2, x

    return moves(step)


EAST = moves(lambda z, yl, core, yh, x: (z, yl, core, yh, x + 1))
WEST = moves(lambda z, yl, core, yh, x: (z, yl, core, yh, x - 1))
NORTH, SOUTH = along_y(1), along_y(-1)
ALONG_X = moves(lambda z, yl, core, yh, x: (z, yl, core, yh, x + 1 - 2 * core))
ACROSS = moves(lambda z, yl, core, yh, x: (z, yl, core, 1 - yh, x))
TWIN = moves(lambda z, yl, core, yh, x: (z, 1 - yl, core, yh, x))
CORE = moves(lambda z, yl, core, yh, x: (z, yl, 1 - core, yh, x))
RING = moves(lambda z, yl, core, yh, x: (z + 1 - 2 * core, yl, core, yh, x))


def send(value, pairs):
    return lax.ppermute(value, AXES, pairs)


def cat(*parts):
    return jnp.concatenate(parts, axis=0)


def place():
    row, col = lax.axis_index("row"), lax.axis_index("col")
    return row // 4, (row // 2) % 2, row % 2, col


def listed(table, a, b):
    return table[jnp.minimum(a, b), jnp.maximum(a, b)] > 0


def mask_kernel(pattern, matrix, masked, keep, away, table, block, sems):
    fetches = [
        pltpu.make_async_copy(pattern, table, sems.at[0]),
        pltpu.make_async_copy(matrix, block, sems.at[1]),
    ]
    for fetch in fetches:
        fetch.start()
    for fetch in fetches:
        fetch.wait()
    _, yl, _, _ = place()

    def body(rows, cols, a, b):
        factor = jnp.where(listed(table, a, b) | (a == b), 1.0, 0.0).astype(F32)
        masked[rows, cols] = (block[rows, cols].astype(F32) * factor).astype(BF16)

    tiles(body)

    @pl.when(yl == 0)
    def _():
        keep[...] = masked[:, :HALF]
        away[...] = masked[:, HALF:]

    @pl.when(yl == 1)
    def _():
        keep[...] = masked[:, HALF:]
        away[...] = masked[:, :HALF]


def tiles(body):
    row, col = lax.axis_index("row"), lax.axis_index("col")
    for i in range(ROWS // SLAB):
        for j in range(COLS // BLOCK):
            rows, cols = slice(SLAB * i, SLAB * (i + 1)), slice(BLOCK * j, BLOCK * (j + 1))
            body(rows, cols, (row * 3 + i) // 2, col * 6 + j)


def fill_left(left, pieces):
    own, w, e, y, x2, yw, ye, y2 = pieces
    _, _, _, col = place()
    yh, x = col // 4, col % 4

    def put(ref, dx, dy):
        index = lax.rem(yh + dy, 2) * 4 + lax.rem(x + dx + 4, 4)
        for core in range(2):
            columns = slice(ROWS * core, ROWS * (core + 1))
            left[index, core] = ref[:, columns]

    put(own, 0, 0)
    put(w, -1, 0)
    put(e, 1, 0)
    put(y, 0, 1)
    put(x2, 2, 0)
    put(yw, -1, 1)
    put(ye, 1, 1)
    put(y2, 2, 1)


def multiply(left, rows, parts):
    def part(k, core, ref, first):
        return jnp.dot(
            left[lax.rem(k + 16, 8), core, rows], ref[first : first + ROWS, :], preferred_element_type=F32
        )

    return sum((part(*p) for p in parts[1:]), part(*parts[0]))


def near_sums(left, pieces):
    z, _, core, _ = place()
    sign = 2 * core - 1
    parts = []
    for s in range(4):
        parts.append((z + sign * s, core, pieces[2 * s], 0))
        parts.append((z + sign * s, 1 - core, pieces[2 * s + 1], 0))
    return multiply(left, slice(0, HALF), parts)


def square_kernel(*refs):
    total, left = refs[16:]
    fill_left(left, refs[:8])
    total[...] = near_sums(left, refs[8:16])


def update_kernel(*refs):
    refs[9][...] = near_sums(refs[0], refs[1:9])


def last_kernel(half, left, total, a4, *refs):
    *far, s4, result = refs
    z, _, core, _ = place()
    sign = 2 * core - 1
    rows = slice(ROWS * half, ROWS * (half + 1))
    parts = [(z + 4, core, a4, 0), (z + 4, 1 - core, s4, 0)]
    swapped = [(ref, first) for ref in far for first in range(0, ref.shape[0], 2 * ROWS)]
    for s, (ref, first) in enumerate(swapped):
        parts.append((z - sign * (s + 1), 1 - core, ref, first))
        parts.append((z - sign * (s + 1), core, ref, first + ROWS))
    result[...] = (total[rows] + multiply(left, rows, parts)).astype(result.dtype)


def factor_kernel(pattern, keep, kept_square, eye, kept_result):
    row, col = lax.axis_index("row"), lax.axis_index("col")

    def body(rows, cols, a, b):
        shape = (SLAB, BLOCK)
        down = lax.broadcasted_iota(jnp.int32, shape, 0) + (row * ROWS + rows.start)
        over = lax.broadcasted_iota(jnp.int32, shape, 1) + (col * COLS + cols.start)
        eye[rows, cols] = jnp.where(down == over, 1.5, 0.0).astype(F32)
        square_factor = jnp.where(listed(keep, a, b), 0.5, 0.0).astype(F32)
        kept_square[rows, cols] = jnp.full(shape, square_factor, F32)
        result_factor = jnp.where(listed(pattern, a, b) | (a == b), 1.0, 0.0).astype(F32)
        kept_result[rows, cols] = jnp.full(shape, result_factor, F32)

    tiles(body)


SMEM, VMEM = (pl.BlockSpec(memory_space=space) for space in (pltpu.SMEM, pltpu.VMEM))


def struct(*shape, dtype=BF16):
    return jax.ShapeDtypeStruct(shape, dtype)


def call(kernel, args, outs, scratch, flops, specs=None):
    return pl.pallas_call(
        kernel,
        in_specs=specs or [SMEM if arg.dtype == jnp.int32 else VMEM for arg in args],
        out_specs=[VMEM] * len(outs),
        out_shape=outs,
        scratch_shapes=scratch,
        cost_estimate=pl.CostEstimate(flops=flops, bytes_accessed=0, transcendentals=0),
        compiler_params=pltpu.CompilerParams(vmem_limit_bytes=VMEM_LIMIT),
    )(*args)


def after(value, *others):
    return lax.optimization_barrier((value, *others))[0]


def ring(piece, multiply_by, **awaited):
    def step(value, name):
        return send(after(value, *awaited.get(name, ())), RING)

    other = send(piece, CORE)
    a1, b1 = step(piece, "a1"), step(other, "b1")
    a2, b2 = step(a1, "a2"), step(b1, "b2")
    a3, b3 = step(a2, "a3"), step(b2, "b3")
    a4 = step(a3, "a4")
    sums = multiply_by([piece, other, a1, b1, a2, b2, a3, b3])
    far = [send(cat(a1, b1), CORE), send(after(cat(a2, b2), *awaited.get("s2", ())), CORE), send(cat(a3, b3), CORE)]
    return sums, [a4, *far, send(after(a4, sums[0]), CORE)]


def row(piece):
    w, e, y = send(piece, EAST), send(piece, WEST), send(piece, ACROSS)
    x2 = send(jnp.where(place()[2] == 0, w, e), ALONG_X)
    yw, ye = send(y, EAST), send(y, WEST)
    return [piece, w, e, y, x2, yw, ye, send(x2, ACROSS)]


FLOPS = 2 * ROWS * COLS * 6144
SUMS = struct(HALF, COLS, dtype=F32)


def sums(left, total, last):
    args = [left, total, *last]
    away_kernel, keep_kernel = functools.partial(last_kernel, 1), functools.partial(last_kernel, 0)
    (away,) = call(away_kernel, args, [struct(ROWS, COLS)], [], FLOPS // 4)
    theirs = send(away, TWIN)
    (kept,) = call(keep_kernel, args, [struct(ROWS, COLS, dtype=F32)], [], FLOPS // 4)
    return kept + theirs.astype(F32)


def in_hbm(value):
    return pltpu.with_memory_space_constraint(value, pltpu.HBM)


def shards(matrix, pattern, keep):
    x, kept, away = call(
        mask_kernel,
        [in_hbm(pattern), in_hbm(matrix)],
        [struct(ROWS, COLS), struct(ROWS, HALF), struct(ROWS, HALF)],
        [pltpu.SMEM((48, 48), jnp.int32), pltpu.VMEM((ROWS, COLS), BF16), pltpu.SemaphoreType.DMA((2,))],
        0,
        [pl.BlockSpec(memory_space=pltpu.HBM)] * 2,
    )
    kept_square, eye, kept_result = call(
        factor_kernel, [pattern, keep], [struct(ROWS, COLS, dtype=F32)] * 3, [], ROWS * COLS
    )
    pieces = row(cat(kept, send(away, TWIN)))

    def square(near):
        return call(square_kernel, [*pieces, *near], [SUMS, struct(8, 2, HALF, ROWS)], [], FLOPS // 2)

    (total, left), last = ring(x, square, a2=pieces[:1], a3=pieces[1:4], b3=pieces[4:5], s2=pieces[5:])
    weight = (eye - sums(left, total, last) * kept_square).astype(BF16)

    def update(near):
        return call(update_kernel, [left, *near], [SUMS], [], FLOPS // 2)

    (total,), last = ring(weight, update)
    return (sums(left, total, last) * kept_result).astype(BF16)


def solution(mesh):
    return jax.shard_map(
        shards,
        mesh=mesh,
        in_specs=(P("row", "col"), P(), P()),
        out_specs=P("row", "col"),
        check_vma=False,
    )
```

```python
import functools

import jax
import jax.numpy as jnp
import numpy as np
from jax import lax
from jax.experimental import pallas as pl
from jax.experimental.pallas import tpu as pltpu
from jax.sharding import PartitionSpec as P

SIZES = (8, 2, 2, 2, 4)
AXES = ("row", "col")
ROWS, COLS = 192, 768
HALF = COLS // 2
SLAB, BLOCK = 64, 128
VMEM_LIMIT = 18 * 1024 * 1024
F32, BF16 = jnp.float32, jnp.bfloat16


def moves(step):
    pairs = []
    for index, place in enumerate(np.ndindex(*SIZES)):
        target = np.mod(step(*place), SIZES)
        pairs.append((index, int(np.ravel_multi_index(target, SIZES))))
    return pairs


def along_y(sign):
    def step(z, yl, core, yh, x):
        y = (2 * yh + yl + sign) % 4
        return z, y % 2, core, y // 2, x

    return moves(step)


EAST = moves(lambda z, yl, core, yh, x: (z, yl, core, yh, x + 1))
WEST = moves(lambda z, yl, core, yh, x: (z, yl, core, yh, x - 1))
NORTH, SOUTH = along_y(1), along_y(-1)
ALONG_X = moves(lambda z, yl, core, yh, x: (z, yl, core, yh, x + 1 - 2 * core))
ACROSS = moves(lambda z, yl, core, yh, x: (z, yl, core, 1 - yh, x))
TWIN = moves(lambda z, yl, core, yh, x: (z, 1 - yl, core, yh, x))
CORE = moves(lambda z, yl, core, yh, x: (z, yl, 1 - core, yh, x))
RING = moves(lambda z, yl, core, yh, x: (z + 1 - 2 * core, yl, core, yh, x))


def send(value, pairs):
    return lax.ppermute(value, AXES, pairs)


def cat(*parts):
    return jnp.concatenate(parts, axis=0)


def place():
    row, col = lax.axis_index("row"), lax.axis_index("col")
    return row // 4, (row // 2) % 2, row % 2, col


def listed(table, a, b):
    return table[jnp.minimum(a, b), jnp.maximum(a, b)] > 0


def mask_kernel(pattern, matrix, masked, keep, away, table, block, sems):
    fetches = [
        pltpu.make_async_copy(pattern, table, sems.at[0]),
        pltpu.make_async_copy(matrix, block, sems.at[1]),
    ]
    for fetch in fetches:
        fetch.start()
    for fetch in fetches:
        fetch.wait()
    _, yl, _, _ = place()

    def body(rows, cols, a, b):
        factor = jnp.where(listed(table, a, b) | (a == b), 1.0, 0.0).astype(F32)
        masked[rows, cols] = (block[rows, cols].astype(F32) * factor).astype(BF16)

    tiles(body)

    @pl.when(yl == 0)
    def _():
        keep[...] = masked[:, :HALF]
        away[...] = masked[:, HALF:]

    @pl.when(yl == 1)
    def _():
        keep[...] = masked[:, HALF:]
        away[...] = masked[:, :HALF]


def tiles(body):
    row, col = lax.axis_index("row"), lax.axis_index("col")
    for i in range(ROWS // SLAB):
        for j in range(COLS // BLOCK):
            rows, cols = slice(SLAB * i, SLAB * (i + 1)), slice(BLOCK * j, BLOCK * (j + 1))
            body(rows, cols, (row * 3 + i) // 2, col * 6 + j)


def fill_left(left, pieces):
    own, w, e, y, x2, yw, ye, y2 = pieces
    _, _, _, col = place()
    yh, x = col // 4, col % 4

    def put(ref, dx, dy):
        index = lax.rem(yh + dy, 2) * 4 + lax.rem(x + dx + 4, 4)
        for core in range(2):
            columns = slice(ROWS * core, ROWS * (core + 1))
            left[index, core] = ref[:, columns]

    put(own, 0, 0)
    put(w, -1, 0)
    put(e, 1, 0)
    put(y, 0, 1)
    put(x2, 2, 0)
    put(yw, -1, 1)
    put(ye, 1, 1)
    put(y2, 2, 1)


def multiply(left, rows, parts):
    def part(k, core, ref, first):
        return jnp.dot(
            left[lax.rem(k + 16, 8), core, rows], ref[first : first + ROWS, :], preferred_element_type=F32
        )

    return sum((part(*p) for p in parts[1:]), part(*parts[0]))


def near_sums(left, pieces):
    z, _, core, _ = place()
    sign = 2 * core - 1
    parts = []
    for s in range(4):
        parts.append((z + sign * s, core, pieces[2 * s], 0))
        parts.append((z + sign * s, 1 - core, pieces[2 * s + 1], 0))
    return multiply(left, slice(0, HALF), parts)


def square_kernel(*refs):
    total, left = refs[16:]
    fill_left(left, refs[:8])
    total[...] = near_sums(left, refs[8:16])


def update_kernel(*refs):
    refs[9][...] = near_sums(refs[0], refs[1:9])


def last_kernel(half, left, total, a4, *refs):
    *far, s4, result = refs
    z, _, core, _ = place()
    sign = 2 * core - 1
    rows = slice(ROWS * half, ROWS * (half + 1))
    parts = [(z + 4, core, a4, 0), (z + 4, 1 - core, s4, 0)]
    swapped = [(ref, first) for ref in far for first in range(0, ref.shape[0], 2 * ROWS)]
    for s, (ref, first) in enumerate(swapped):
        parts.append((z - sign * (s + 1), 1 - core, ref, first))
        parts.append((z - sign * (s + 1), core, ref, first + ROWS))
    result[...] = (total[rows] + multiply(left, rows, parts)).astype(result.dtype)


def factor_kernel(pattern, keep, kept_square, eye, kept_result):
    row, col = lax.axis_index("row"), lax.axis_index("col")

    def body(rows, cols, a, b):
        shape = (SLAB, BLOCK)
        down = lax.broadcasted_iota(jnp.int32, shape, 0) + (row * ROWS + rows.start)
        over = lax.broadcasted_iota(jnp.int32, shape, 1) + (col * COLS + cols.start)
        eye[rows, cols] = jnp.where(down == over, 1.5, 0.0).astype(F32).astype(BF16)
        square_factor = jnp.where(listed(keep, a, b), 0.5, 0.0).astype(F32)
        kept_square[rows, cols] = jnp.full(shape, square_factor, F32).astype(BF16)
        result_factor = jnp.where(listed(pattern, a, b) | (a == b), 1.0, 0.0).astype(F32)
        kept_result[rows, cols] = jnp.full(shape, result_factor, F32).astype(BF16)

    tiles(body)


SMEM, VMEM = (pl.BlockSpec(memory_space=space) for space in (pltpu.SMEM, pltpu.VMEM))


def struct(*shape, dtype=BF16):
    return jax.ShapeDtypeStruct(shape, dtype)


def call(kernel, args, outs, scratch, flops, specs=None):
    return pl.pallas_call(
        kernel,
        in_specs=specs or [SMEM if arg.dtype == jnp.int32 else VMEM for arg in args],
        out_specs=[VMEM] * len(outs),
        out_shape=outs,
        scratch_shapes=scratch,
        cost_estimate=pl.CostEstimate(flops=flops, bytes_accessed=0, transcendentals=0),
        compiler_params=pltpu.CompilerParams(vmem_limit_bytes=VMEM_LIMIT),
    )(*args)


def after(value, *others):
    return lax.optimization_barrier((value, *others))[0]


def ring(piece, multiply_by, **awaited):
    def step(value, name):
        return send(after(value, *awaited.get(name, ())), RING)

    other = send(piece, CORE)
    a1, b1 = step(piece, "a1"), step(other, "b1")
    a2, b2 = step(a1, "a2"), step(b1, "b2")
    a3, b3 = step(a2, "a3"), step(b2, "b3")
    a4 = step(a3, "a4")
    sums = multiply_by([piece, other, a1, b1, a2, b2, a3, b3])
    far = [send(cat(a1, b1), CORE), send(after(cat(a2, b2), *awaited.get("s2", ())), CORE), send(cat(a3, b3), CORE)]
    return sums, [a4, *far, send(after(a4, sums[0]), CORE)]


def row(piece):
    w, e, y = send(piece, EAST), send(piece, WEST), send(piece, ACROSS)
    x2 = send(jnp.where(place()[2] == 0, w, e), ALONG_X)
    yw, ye = send(y, EAST), send(y, WEST)
    return [piece, w, e, y, x2, yw, ye, send(x2, ACROSS)]


FLOPS = 2 * ROWS * COLS * 6144
SUMS = struct(HALF, COLS, dtype=F32)


def sums(left, total, last):
    args = [left, total, *last]
    away_kernel, keep_kernel = functools.partial(last_kernel, 1), functools.partial(last_kernel, 0)
    (away,) = call(away_kernel, args, [struct(ROWS, COLS)], [], FLOPS // 4)
    theirs = send(away, TWIN)
    (kept,) = call(keep_kernel, args, [struct(ROWS, COLS, dtype=F32)], [], FLOPS // 4)
    return kept + theirs.astype(F32)


def in_hbm(value):
    return pltpu.with_memory_space_constraint(value, pltpu.HBM)


def shards(matrix, pattern, keep):
    x, kept, away = call(
        mask_kernel,
        [in_hbm(pattern), in_hbm(matrix)],
        [struct(ROWS, COLS), struct(ROWS, HALF), struct(ROWS, HALF)],
        [pltpu.SMEM((48, 48), jnp.int32), pltpu.VMEM((ROWS, COLS), BF16), pltpu.SemaphoreType.DMA((2,))],
        0,
        [pl.BlockSpec(memory_space=pltpu.HBM)] * 2,
    )
    kept_square, eye, kept_result = call(
        factor_kernel, [pattern, keep], [struct(ROWS, COLS)] * 3, [], ROWS * COLS
    )
    pieces = row(cat(kept, send(away, TWIN)))

    def square(near):
        return call(square_kernel, [*pieces, *near], [SUMS, struct(8, 2, HALF, ROWS)], [], FLOPS // 2)

    (total, left), last = ring(x, square, a2=pieces[:1], a3=pieces[1:4], b3=pieces[4:5], s2=pieces[5:])
    weight = (eye - sums(left, total, last) * kept_square).astype(BF16)

    def update(near):
        return call(update_kernel, [left, *near], [SUMS], [], FLOPS // 2)

    (total,), last = ring(weight, update)
    return (sums(left, total, last) * kept_result).astype(BF16)


def solution(mesh):
    return jax.shard_map(
        shards,
        mesh=mesh,
        in_specs=(P("row", "col"), P(), P()),
        out_specs=P("row", "col"),
        check_vma=False,
    )
```

```python
import functools

import jax
import jax.numpy as jnp
import numpy as np
from jax import lax
from jax.experimental import pallas as pl
from jax.experimental.pallas import tpu as pltpu
from jax.sharding import PartitionSpec as P

SIZES = (8, 2, 2, 2, 4)
AXES = ("row", "col")
ROWS, COLS = 192, 768
HALF = COLS // 2
SLAB, BLOCK = 64, 128
VMEM_LIMIT = 18 * 1024 * 1024
F32, BF16 = jnp.float32, jnp.bfloat16


def moves(step):
    pairs = []
    for index, place in enumerate(np.ndindex(*SIZES)):
        target = np.mod(step(*place), SIZES)
        pairs.append((index, int(np.ravel_multi_index(target, SIZES))))
    return pairs


def along_y(sign):
    def step(z, yl, core, yh, x):
        y = (2 * yh + yl + sign) % 4
        return z, y % 2, core, y // 2, x

    return moves(step)


EAST = moves(lambda z, yl, core, yh, x: (z, yl, core, yh, x + 1))
WEST = moves(lambda z, yl, core, yh, x: (z, yl, core, yh, x - 1))
NORTH, SOUTH = along_y(1), along_y(-1)
ALONG_X = moves(lambda z, yl, core, yh, x: (z, yl, core, yh, x + 1 - 2 * core))
ACROSS = moves(lambda z, yl, core, yh, x: (z, yl, core, 1 - yh, x))
TWIN = moves(lambda z, yl, core, yh, x: (z, 1 - yl, core, yh, x))
CORE = moves(lambda z, yl, core, yh, x: (z, yl, 1 - core, yh, x))
RING = moves(lambda z, yl, core, yh, x: (z + 1 - 2 * core, yl, core, yh, x))


def send(value, pairs):
    return lax.ppermute(value, AXES, pairs)


def cat(*parts):
    return jnp.concatenate(parts, axis=0)


def place():
    row, col = lax.axis_index("row"), lax.axis_index("col")
    return row // 4, (row // 2) % 2, row % 2, col


def listed(table, a, b):
    return table[jnp.minimum(a, b), jnp.maximum(a, b)] > 0


def mask_kernel(pattern, matrix, masked, keep, away, table, block, sems):
    fetches = [
        pltpu.make_async_copy(pattern, table, sems.at[0]),
        pltpu.make_async_copy(matrix, block, sems.at[1]),
    ]
    for fetch in fetches:
        fetch.start()
    for fetch in fetches:
        fetch.wait()
    _, yl, _, _ = place()

    def body(rows, cols, a, b):
        factor = jnp.where(listed(table, a, b) | (a == b), 1.0, 0.0).astype(F32)
        masked[rows, cols] = (block[rows, cols].astype(F32) * factor).astype(BF16)

    tiles(body)

    @pl.when(yl == 0)
    def _():
        keep[...] = masked[:, :HALF]
        away[...] = masked[:, HALF:]

    @pl.when(yl == 1)
    def _():
        keep[...] = masked[:, HALF:]
        away[...] = masked[:, :HALF]


def tiles(body):
    row, col = lax.axis_index("row"), lax.axis_index("col")
    for i in range(ROWS // SLAB):
        for j in range(COLS // BLOCK):
            rows, cols = slice(SLAB * i, SLAB * (i + 1)), slice(BLOCK * j, BLOCK * (j + 1))
            body(rows, cols, (row * 3 + i) // 2, col * 6 + j)


def fill_left(left, pieces):
    own, w, e, y, x2, yw, ye, y2 = pieces
    _, _, _, col = place()
    yh, x = col // 4, col % 4

    def put(ref, dx, dy):
        index = lax.rem(yh + dy, 2) * 4 + lax.rem(x + dx + 4, 4)
        for core in range(2):
            columns = slice(ROWS * core, ROWS * (core + 1))
            left[index, core] = ref[:, columns]

    put(own, 0, 0)
    put(w, -1, 0)
    put(e, 1, 0)
    put(y, 0, 1)
    put(x2, 2, 0)
    put(yw, -1, 1)
    put(ye, 1, 1)
    put(y2, 2, 1)


def multiply(left, rows, parts):
    def part(k, core, ref, first):
        return jnp.dot(
            left[lax.rem(k + 16, 8), core, rows], ref[first : first + ROWS, :], preferred_element_type=F32
        )

    return sum((part(*p) for p in parts[1:]), part(*parts[0]))


def near_sums(left, pieces):
    z, _, core, _ = place()
    sign = 2 * core - 1
    parts = []
    for s in range(4):
        parts.append((z + sign * s, core, pieces[2 * s], 0))
        parts.append((z + sign * s, 1 - core, pieces[2 * s + 1], 0))
    return multiply(left, slice(0, HALF), parts)


def square_kernel(*refs):
    total, left = refs[16:]
    fill_left(left, refs[:8])
    total[...] = near_sums(left, refs[8:16])


def update_kernel(*refs):
    refs[9][...] = near_sums(refs[0], refs[1:9])


def last_kernel(half, left, total, a4, *refs):
    *far, s4, result = refs
    z, _, core, _ = place()
    sign = 2 * core - 1
    rows = slice(ROWS * half, ROWS * (half + 1))
    parts = [(z + 4, core, a4, 0), (z + 4, 1 - core, s4, 0)]
    swapped = [(ref, first) for ref in far for first in range(0, ref.shape[0], 2 * ROWS)]
    for s, (ref, first) in enumerate(swapped):
        parts.append((z - sign * (s + 1), 1 - core, ref, first))
        parts.append((z - sign * (s + 1), core, ref, first + ROWS))
    result[...] = (total[rows] + multiply(left, rows, parts)).astype(result.dtype)


def keep_kernel(left, total, scale, offset, *refs):
    result = refs[-1]
    last_kernel(0, left, total, *refs)
    result[...] = offset[...] + scale[...] * result[...]


def factor_kernel(pattern, keep, kept_square, eye, kept_result):
    row, col = lax.axis_index("row"), lax.axis_index("col")

    def body(rows, cols, a, b):
        shape = (SLAB, BLOCK)
        down = lax.broadcasted_iota(jnp.int32, shape, 0) + (row * ROWS + rows.start)
        over = lax.broadcasted_iota(jnp.int32, shape, 1) + (col * COLS + cols.start)
        eye[rows, cols] = jnp.where(down == over, 1.5, 0.0).astype(F32)
        square_factor = jnp.where(listed(keep, a, b), -0.5, 0.0).astype(F32)
        kept_square[rows, cols] = jnp.full(shape, square_factor, F32)
        result_factor = jnp.where(listed(pattern, a, b) | (a == b), 1.0, 0.0).astype(F32)
        kept_result[rows, cols] = jnp.full(shape, result_factor, F32)

    tiles(body)


SMEM, VMEM = (pl.BlockSpec(memory_space=space) for space in (pltpu.SMEM, pltpu.VMEM))


def struct(*shape, dtype=BF16):
    return jax.ShapeDtypeStruct(shape, dtype)


def call(kernel, args, outs, scratch, flops, specs=None):
    return pl.pallas_call(
        kernel,
        in_specs=specs or [SMEM if arg.dtype == jnp.int32 else VMEM for arg in args],
        out_specs=[VMEM] * len(outs),
        out_shape=outs,
        scratch_shapes=scratch,
        cost_estimate=pl.CostEstimate(flops=flops, bytes_accessed=0, transcendentals=0),
        compiler_params=pltpu.CompilerParams(vmem_limit_bytes=VMEM_LIMIT),
    )(*args)


def after(value, *others):
    return lax.optimization_barrier((value, *others))[0]


def ring(piece, multiply_by, **awaited):
    def step(value, name):
        return send(after(value, *awaited.get(name, ())), RING)

    other = send(piece, CORE)
    a1, b1 = step(piece, "a1"), step(other, "b1")
    a2, b2 = step(a1, "a2"), step(b1, "b2")
    a3, b3 = step(a2, "a3"), step(b2, "b3")
    a4 = step(a3, "a4")
    sums = multiply_by([piece, other, a1, b1, a2, b2, a3, b3])
    far = [send(cat(a1, b1), CORE), send(after(cat(a2, b2), *awaited.get("s2", ())), CORE), send(cat(a3, b3), CORE)]
    return sums, [a4, *far, send(after(a4, sums[0]), CORE)]


def row(piece):
    w, e, y = send(piece, EAST), send(piece, WEST), send(piece, ACROSS)
    x2 = send(jnp.where(place()[2] == 0, w, e), ALONG_X)
    yw, ye = send(y, EAST), send(y, WEST)
    return [piece, w, e, y, x2, yw, ye, send(x2, ACROSS)]


FLOPS = 2 * ROWS * COLS * 6144
SUMS = struct(HALF, COLS, dtype=F32)


def scaled_sums(left, total, last, scale, offset):
    (away,) = call(
        functools.partial(last_kernel, 1), [left, total, *last], [struct(ROWS, COLS)], [], FLOPS // 4
    )
    theirs = send(away, TWIN)
    args = [left, total, scale, offset, *last]
    (kept,) = call(keep_kernel, args, [struct(ROWS, COLS, dtype=F32)], [], FLOPS // 4)
    return (kept + scale * theirs.astype(F32)).astype(BF16)


def in_hbm(value):
    return pltpu.with_memory_space_constraint(value, pltpu.HBM)


def shards(matrix, pattern, keep):
    x, kept, away = call(
        mask_kernel,
        [in_hbm(pattern), in_hbm(matrix)],
        [struct(ROWS, COLS), struct(ROWS, HALF), struct(ROWS, HALF)],
        [pltpu.SMEM((48, 48), jnp.int32), pltpu.VMEM((ROWS, COLS), BF16), pltpu.SemaphoreType.DMA((2,))],
        0,
        [pl.BlockSpec(memory_space=pltpu.HBM)] * 2,
    )
    kept_square, eye, kept_result = call(
        factor_kernel, [pattern, keep], [struct(ROWS, COLS, dtype=F32)] * 3, [], ROWS * COLS
    )
    pieces = row(cat(kept, send(away, TWIN)))

    def square(near):
        return call(square_kernel, [*pieces, *near], [SUMS, struct(8, 2, HALF, ROWS)], [], FLOPS // 2)

    (total, left), last = ring(x, square, a2=pieces[:1], a3=pieces[1:4], b3=pieces[4:5], s2=pieces[5:])
    weight = scaled_sums(left, total, last, kept_square, eye)

    def update(near):
        return call(update_kernel, [left, *near], [SUMS], [], FLOPS // 2)

    (total,), last = ring(weight, update)
    return scaled_sums(left, total, last, kept_result, jnp.zeros_like(eye))


def solution(mesh):
    return jax.shard_map(
        shards,
        mesh=mesh,
        in_specs=(P("row", "col"), P(), P()),
        out_specs=P("row", "col"),
        check_vma=False,
    )
```

```python
import functools

import jax
import jax.numpy as jnp
import numpy as np
from jax import lax
from jax.experimental import pallas as pl
from jax.experimental.pallas import tpu as pltpu
from jax.sharding import PartitionSpec as P

SIZES = (8, 2, 2, 2, 4)
AXES = ("row", "col")
ROWS, COLS = 192, 768
HALF = COLS // 2
SLAB, BLOCK = 64, 128
VMEM_LIMIT = 18 * 1024 * 1024
F32, BF16 = jnp.float32, jnp.bfloat16


def moves(step):
    pairs = []
    for index, place in enumerate(np.ndindex(*SIZES)):
        target = np.mod(step(*place), SIZES)
        pairs.append((index, int(np.ravel_multi_index(target, SIZES))))
    return pairs


def along_y(sign):
    def step(z, yl, core, yh, x):
        y = (2 * yh + yl + sign) % 4
        return z, y % 2, core, y // 2, x

    return moves(step)


EAST = moves(lambda z, yl, core, yh, x: (z, yl, core, yh, x + 1))
WEST = moves(lambda z, yl, core, yh, x: (z, yl, core, yh, x - 1))
NORTH, SOUTH = along_y(1), along_y(-1)
ALONG_X = moves(lambda z, yl, core, yh, x: (z, yl, core, yh, x + 1 - 2 * core))
ACROSS = moves(lambda z, yl, core, yh, x: (z, yl, core, 1 - yh, x))
TWIN = moves(lambda z, yl, core, yh, x: (z, 1 - yl, core, yh, x))
CORE = moves(lambda z, yl, core, yh, x: (z, yl, 1 - core, yh, x))
RING = moves(lambda z, yl, core, yh, x: (z + 1 - 2 * core, yl, core, yh, x))


def send(value, pairs):
    return lax.ppermute(value, AXES, pairs)


def cat(*parts):
    return jnp.concatenate(parts, axis=0)


def place():
    row, col = lax.axis_index("row"), lax.axis_index("col")
    return row // 4, (row // 2) % 2, row % 2, col


def listed(table, a, b):
    return table[jnp.minimum(a, b), jnp.maximum(a, b)] > 0


def mask_kernel(pattern, matrix, masked, keep, away, table, block, sems):
    fetches = [
        pltpu.make_async_copy(pattern, table, sems.at[0]),
        pltpu.make_async_copy(matrix, block, sems.at[1]),
    ]
    for fetch in fetches:
        fetch.start()
    for fetch in fetches:
        fetch.wait()
    _, yl, _, _ = place()

    def body(rows, cols, a, b):
        factor = jnp.where(listed(table, a, b) | (a == b), 1.0, 0.0).astype(F32)
        masked[rows, cols] = (block[rows, cols].astype(F32) * factor).astype(BF16)

    tiles(body)

    @pl.when(yl == 0)
    def _():
        keep[...] = masked[:, :HALF]
        away[...] = masked[:, HALF:]

    @pl.when(yl == 1)
    def _():
        keep[...] = masked[:, HALF:]
        away[...] = masked[:, :HALF]


def tiles(body):
    row, col = lax.axis_index("row"), lax.axis_index("col")
    for i in range(ROWS // SLAB):
        for j in range(COLS // BLOCK):
            rows, cols = slice(SLAB * i, SLAB * (i + 1)), slice(BLOCK * j, BLOCK * (j + 1))
            body(rows, cols, (row * 3 + i) // 2, col * 6 + j)


def fill_left(left, pieces):
    own, w, e, y, x2, yw, ye, y2 = pieces
    _, _, _, col = place()
    yh, x = col // 4, col % 4

    def put(ref, dx, dy):
        index = lax.rem(yh + dy, 2) * 4 + lax.rem(x + dx + 4, 4)
        for core in range(2):
            columns = slice(ROWS * core, ROWS * (core + 1))
            left[index, core] = ref[:, columns]

    put(own, 0, 0)
    put(w, -1, 0)
    put(e, 1, 0)
    put(y, 0, 1)
    put(x2, 2, 0)
    put(yw, -1, 1)
    put(ye, 1, 1)
    put(y2, 2, 1)


def multiply(left, rows, parts):
    def part(k, core, ref, first):
        return jnp.dot(
            left[lax.rem(k + 16, 8), core, rows], ref[first : first + ROWS, :], preferred_element_type=F32
        )

    return sum((part(*p) for p in parts[1:]), part(*parts[0]))


def near_sums(left, pieces):
    z, _, core, _ = place()
    sign = 2 * core - 1
    parts = []
    for s in range(4):
        parts.append((z + sign * s, core, pieces[2 * s], 0))
        parts.append((z + sign * s, 1 - core, pieces[2 * s + 1], 0))
    return multiply(left, slice(0, HALF), parts)


def square_kernel(*refs):
    total, left = refs[16:]
    fill_left(left, refs[:8])
    total[...] = near_sums(left, refs[8:16])


def update_kernel(*refs):
    refs[9][...] = near_sums(refs[0], refs[1:9])


def last_kernel(half, left, total, a4, *refs):
    *far, s4, result = refs
    z, _, core, _ = place()
    sign = 2 * core - 1
    rows = slice(ROWS * half, ROWS * (half + 1))
    parts = [(z + 4, core, a4, 0), (z + 4, 1 - core, s4, 0)]
    swapped = [(ref, first) for ref in far for first in range(0, ref.shape[0], 2 * ROWS)]
    for s, (ref, first) in enumerate(swapped):
        parts.append((z - sign * (s + 1), 1 - core, ref, first))
        parts.append((z - sign * (s + 1), core, ref, first + ROWS))
    result[...] = (total[rows] + multiply(left, rows, parts)).astype(result.dtype)


def factor_kernel(pattern, keep, kept_square, eye, kept_result):
    row, col = lax.axis_index("row"), lax.axis_index("col")

    def body(rows, cols, a, b):
        shape = (SLAB, BLOCK)
        down = lax.broadcasted_iota(jnp.int32, shape, 0) + (row * ROWS + rows.start)
        over = lax.broadcasted_iota(jnp.int32, shape, 1) + (col * COLS + cols.start)
        eye[rows, cols] = jnp.where(down == over, 1.5, 0.0).astype(F32)
        square_factor = jnp.where(listed(keep, a, b), 0.5, 0.0).astype(F32)
        kept_square[rows, cols] = jnp.full(shape, square_factor, F32)
        result_factor = jnp.where(listed(pattern, a, b) | (a == b), 1.0, 0.0).astype(F32)
        kept_result[rows, cols] = jnp.full(shape, result_factor, F32)

    tiles(body)


SMEM, VMEM = (pl.BlockSpec(memory_space=space) for space in (pltpu.SMEM, pltpu.VMEM))


def struct(*shape, dtype=BF16):
    return jax.ShapeDtypeStruct(shape, dtype)


def call(kernel, args, outs, scratch, flops, specs=None):
    return pl.pallas_call(
        kernel,
        in_specs=specs or [SMEM if arg.dtype == jnp.int32 else VMEM for arg in args],
        out_specs=[VMEM] * len(outs),
        out_shape=outs,
        scratch_shapes=scratch,
        cost_estimate=pl.CostEstimate(flops=flops, bytes_accessed=0, transcendentals=0),
        compiler_params=pltpu.CompilerParams(vmem_limit_bytes=VMEM_LIMIT),
    )(*args)


def after(value, *others):
    return lax.optimization_barrier((value, *others))[0]


def ring(piece, multiply_by, **awaited):
    def step(value, name):
        return send(after(value, *awaited.get(name, ())), RING)

    other = send(piece, CORE)
    a1, b1 = step(piece, "a1"), step(other, "b1")
    a2, b2 = step(a1, "a2"), step(b1, "b2")
    a3, b3 = step(a2, "a3"), step(b2, "b3")
    a4 = step(a3, "a4")
    sums = multiply_by([piece, other, a1, b1, a2, b2, a3, b3])
    far = [send(cat(a1, b1), CORE), send(after(cat(a2, b2), *awaited.get("s2", ())), CORE), send(cat(a3, b3), CORE)]
    return sums, [a4, *far, send(after(a4, sums[0]), CORE)]


def row(piece):
    w, e, y = send(piece, EAST), send(piece, WEST), send(piece, ACROSS)
    x2 = send(jnp.where(place()[2] == 0, w, e), ALONG_X)
    yw, ye = send(y, EAST), send(y, WEST)
    return [piece, w, e, y, x2, yw, ye, send(x2, ACROSS)]


FLOPS = 2 * ROWS * COLS * 6144
SUMS = struct(HALF, COLS, dtype=F32)


def sums(left, total, last):
    args = [left, total, *last]
    away_kernel, keep_kernel = functools.partial(last_kernel, 1), functools.partial(last_kernel, 0)
    (away,) = call(away_kernel, args, [struct(ROWS, COLS)], [], FLOPS // 4)
    theirs = send(away, TWIN)
    (kept,) = call(keep_kernel, args, [struct(ROWS, COLS, dtype=F32)], [], FLOPS // 4)
    return kept + theirs.astype(F32)


def in_hbm(value):
    return pltpu.with_memory_space_constraint(value, pltpu.HBM)


def shards(matrix, pattern, keep):
    x, kept, away = call(
        mask_kernel,
        [in_hbm(pattern), in_hbm(matrix)],
        [struct(ROWS, COLS), struct(ROWS, HALF), struct(ROWS, HALF)],
        [pltpu.SMEM((48, 48), jnp.int32), pltpu.VMEM((ROWS, COLS), BF16), pltpu.SemaphoreType.DMA((2,))],
        0,
        [pl.BlockSpec(memory_space=pltpu.HBM)] * 2,
    )
    kept_square, eye, kept_result = call(
        factor_kernel, [pattern, keep], [struct(ROWS, COLS, dtype=F32)] * 3, [], ROWS * COLS
    )
    pieces = row(cat(kept, send(away, TWIN)))

    def square(near):
        return call(square_kernel, [*pieces, *near], [SUMS, struct(8, 2, HALF, ROWS)], [], FLOPS // 2)

    (total, left), last = ring(x, square, a2=pieces[:1], a3=pieces[1:3], b3=pieces[3:5], s2=pieces[5:])
    weight = (eye - sums(left, total, last) * kept_square).astype(BF16)

    def update(near):
        return call(update_kernel, [left, *near], [SUMS], [], FLOPS // 2)

    (total,), last = ring(weight, update)
    return (sums(left, total, last) * kept_result).astype(BF16)


def solution(mesh):
    return jax.shard_map(
        shards,
        mesh=mesh,
        in_specs=(P("row", "col"), P(), P()),
        out_specs=P("row", "col"),
        check_vma=False,
    )
```
